256 devices in a mesh: outer: 16 (over z, x_hi), inner: 16 (over x_lo, y, core).
Axes of the slice: x: 4 (x_hi: 2, x_lo: 2; x = x_hi * 2 + x_lo), y: 4, z: 8, core: 2. Of those that a mesh axis runs over, the one named last changes fastest.
Arguments:
- user_factors: float32 [131072, 256], P(('outer', 'inner')), may hold values from -0.3 to 0.3
- item_factors: float32 [131072, 256], P(('outer', 'inner')), may hold values from -0.3 to 0.3
- ratings: bfloat16 [131072, 8, 512], P(('outer', 'inner')), may hold values from -6 to 6
- weights: bfloat16 [131072, 8, 512], P(('outer', 'inner')), may hold values from 0 to 2, as said below
- tile_list: int32 [256, 8, 4], P(('outer', 'inner')), may hold values from 0 to 3, as said below
- tile_count: int32 [256, 8], P(('outer', 'inner')), may hold values from 1 to 4, as said below
Outputs:
- users_out: float32 [131072, 256], P(('outer', 'inner'))
- items_out: float32 [131072, 256], P(('outer', 'inner'))
The draws below stay inside these ranges and needn't reach their ends.
Inputs may be any that keep to these rules, and one draw needn't show every extreme that they name: Every row tile_list[d,k,:] names each of 0 to 3 once. `tile_count`: in every draw some device lists all 4 tiles in some stratum. `weights`: zero outside the listed tiles and at unobserved entries; elsewhere between 0.5 and 2.
All inputs are finite; a program needn't handle non-finite values.
Results may differ from the reference program's by a relative error of at most 0.003.
Values sent between devices are 32-bit elements; how exact they have to be, the bound alone decides.
A program may use at most 64 MiB of HBM per device.

```python
import jax
import jax.numpy as jnp

R = 256
UD = 512
IB = 512
S_OUT = 2
S_IN = 4
TILES = 4
STRATA = 8
DEVS = 256
USERS = 131072
ITEMS = 131072
N_OUTER = 16
N_INNER = 16


def plan_tiles(key):
    base_key = jax.random.fold_in(key, 7101)
    raw_draw = jax.random.randint(jax.random.fold_in(base_key, 1), (DEVS, STRATA), 0, 16)
    counts = 1 + raw_draw * raw_draw * TILES // 256
    pick_dev = jax.random.randint(jax.random.fold_in(base_key, 2), (), 0, DEVS)
    pick_stratum = jax.random.randint(jax.random.fold_in(base_key, 3), (), 0, STRATA)
    forced = (jnp.arange(DEVS)[:, None] == pick_dev) & (jnp.arange(STRATA)[None, :] == pick_stratum)
    counts = jnp.where(forced, TILES, counts).astype(jnp.int32)
    scores = jax.random.randint(jax.random.fold_in(base_key, 4), (DEVS, STRATA, TILES), 0, 1 << 20) * TILES + jnp.arange(TILES)
    tile_order = jnp.argsort(scores, axis=-1).astype(jnp.int32)
    return (counts, tile_order)


def draw_tile_count(key, part):
    return plan_tiles(key)[0]


def draw_tile_list(key, part):
    return plan_tiles(key)[1]


def draw_weights(key, part):
    counts, tile_order = plan_tiles(key)
    slot_ids = jnp.arange(TILES, dtype=jnp.int32)
    in_list = slot_ids[None, None, :] < counts[:, :, None]
    matched = (tile_order[..., :, None] == slot_ids[None, None, None, :]) & in_list[..., :, None]
    listed = jnp.any(matched, axis=-2).astype(jnp.float32)
    listed = jnp.repeat(listed, IB // TILES, axis=-1)
    observed = jax.random.randint(jax.random.fold_in(key, 8101), (DEVS, UD, STRATA, IB), 0, 2).astype(jnp.float32)
    conf_key = jax.random.fold_in(key, 8102)
    confidence = jax.random.uniform(conf_key, (DEVS, UD, STRATA, IB), jnp.float32, 0.5, 2.0)
    weight = confidence * observed * listed[:, None, :, :]
    return weight.reshape(USERS, STRATA, IB).astype(jnp.bfloat16)


def level_of(key, extent, pieces, least, top_value):
    loudness, own = 1.0, jax.random.fold_in(key, 6)
    for dim, shards_of in pieces:
        draws = jnp.exp(jax.random.uniform(jax.random.fold_in(own, dim), (shards_of,), jnp.float32, least / len(pieces), top_value / len(pieces)))
        loudness = loudness * jnp.repeat(draws, extent[dim] // shards_of).reshape([-1 if axis == dim else 1 for axis in range(len(extent))])
    return loudness


def noise(key, dims, width, most, shards=(), kind=jnp.bfloat16):
    drawn = width * jax.random.normal(key, dims, jnp.float32)
    if shards:
        drawn = drawn * level_of(key, dims, shards, -0.22, 0.18)
    return jnp.clip(drawn, -most, most).astype(kind)


def setup_inputs(seed: int = 0) -> dict:
    arg_keys = jax.random.split(jax.random.key(seed), 7)
    user_factors = jnp.clip(jax.random.uniform(arg_keys[0], (USERS, R), jnp.float32, -0.3, 0.3) * level_of(arg_keys[0], (USERS, R), ((0, 256),), -0.4, 0.0), -0.3, 0.3)
    item_factors = jnp.clip(jax.random.uniform(arg_keys[1], (ITEMS, R), jnp.float32, -0.3, 0.3) * level_of(arg_keys[1], (ITEMS, R), ((0, 256),), -0.4, 0.0), -0.3, 0.3)
    ratings = noise(arg_keys[2], (USERS, STRATA, IB), 1.0, 6.0, ((0, 256),))
    weights = draw_weights(jax.random.fold_in(arg_keys[6], 71), 0)
    tile_list = draw_tile_list(jax.random.fold_in(arg_keys[6], 71), 0)
    tile_count = draw_tile_count(jax.random.fold_in(arg_keys[6], 71), 0)
    return {"user_factors": user_factors, "item_factors": item_factors, "ratings": ratings, "weights": weights, "tile_list": tile_list, "tile_count": tile_count}


learn_rate = 0.015
ridge_weight = 0.05


def listed_columns(tile_list, tile_count):
    slot_ids = jnp.arange(TILES, dtype=jnp.int32)
    in_list = slot_ids[None, :] < tile_count[:, None]
    matched = (tile_list[:, :, None] == slot_ids[None, None, :]) & in_list[:, :, None]
    listed = jnp.any(matched, axis=1).astype(jnp.float32)
    return jnp.repeat(listed, IB // TILES, axis=1)


def reference(user_factors, item_factors, ratings, weights, tile_list, tile_count):
    user_rows = user_factors.reshape(DEVS, UD, R)
    item_rows = item_factors.reshape(DEVS, IB, R)
    for outer_step in range(S_OUT):
        for inner_step in range(S_IN):
            stratum = outer_step * S_IN + inner_step
            tile_mask = listed_columns(tile_list[:, stratum, :], tile_count[:, stratum])
            rating = ratings[:, stratum, :].reshape(DEVS, UD, IB).astype(jnp.float32)
            weight = weights[:, stratum, :].reshape(DEVS, UD, IB).astype(jnp.float32)
            user_half = user_rows.astype(jnp.bfloat16).astype(jnp.float32)
            item_half = item_rows.astype(jnp.bfloat16).astype(jnp.float32)
            predicted = jnp.einsum("dur,dir->dui", user_half, item_half)
            residual = (weight * (predicted - rating) * tile_mask[:, None, :]).astype(jnp.bfloat16).astype(jnp.float32)
            grad_users = jnp.einsum("dui,dir->dur", residual, item_half)
            grad_items = jnp.einsum("dui,dur->dir", residual, user_half)
            user_rows = user_rows - learn_rate * (grad_users + ridge_weight * user_rows)
            item_rows = item_rows - learn_rate * (grad_items + ridge_weight * item_rows)
            grouped = item_rows.reshape(N_OUTER, N_INNER, IB, R)
            if inner_step < S_IN - 1:
                grouped = jnp.roll(grouped, 1, axis=1)
            elif outer_step < S_OUT - 1:
                grouped = jnp.roll(grouped, 1, axis=0)
            item_rows = grouped.reshape(DEVS, IB, R)
    return user_rows.reshape(USERS, R), item_rows.reshape(ITEMS, R)
```

```python
import functools

import jax
import jax.numpy as jnp
from jax import lax
from jax.experimental import pallas as pl
from jax.experimental.pallas import tpu as pltpu
from jax.sharding import PartitionSpec as P

S_OUT = 2
S_IN = 4
STRATA = S_OUT * S_IN
GROUP = 32
PIECES = 2

learn_rate = 0.015
ridge_weight = 0.05

MESH = pl.DeviceIdType.MESH


def listed_scales(list_ref, count_ref, stratum, tile_total):
    count = count_ref[0, stratum]
    scales = []
    for tile in range(tile_total):
        hits = [
            jnp.where(
                (list_ref[0, stratum, slot] == tile) & (slot < count), 1.0, 0.0
            ).astype(jnp.float32)
            for slot in range(tile_total)
        ]
        scales.append(functools.reduce(jnp.maximum, hits))
    return scales


def kernel(
    outer_size,
    inner_size,
    list_ref,
    count_ref,
    user_hbm,
    item_hbm,
    rating_hbm,
    weight_hbm,
    user_out,
    item_out,
    raw,
    sorted_rows,
    user,
    user_half,
    grad_user,
    held,
    fresh,
    load_sem,
    factor_sem,
    send_sem,
    recv_sem,
):
    users, rank = user.shape
    items = held.shape[1]
    width = items // PIECES
    tile_total = list_ref.shape[2]
    tile_width = items // tile_total
    groups = users // GROUP
    group_rows = GROUP * STRATA

    g = lax.axis_index("outer")
    i = lax.axis_index("inner")

    def along(steps_outer, steps_inner):
        return (
            lax.rem(g + steps_outer + outer_size, outer_size),
            lax.rem(i + steps_inner + inner_size, inner_size),
        )

    def load(group, which):
        rows = pl.ds(pl.multiple_of(group * group_rows, group_rows), group_rows)
        source = (rating_hbm, weight_hbm)[which]
        return pltpu.make_async_copy(
            source.at[rows], raw.at[which, rows], load_sem.at[which, group]
        )

    def load_all(group, carry):
        load(group, 0).start()
        load(group, 1).start()
        return carry

    user_load = pltpu.make_async_copy(user_hbm, user, factor_sem.at[0])
    item_load = pltpu.make_async_copy(item_hbm, held.at[0], factor_sem.at[1])
    user_load.start()
    item_load.start()
    lax.fori_loop(0, groups, load_all, 0)

    barrier = pltpu.get_barrier_semaphore()
    for partner in (along(0, 1), along(0, -1), along(1, 0), along(-1, 0)):
        pl.semaphore_signal(barrier, inc=1, device_id=partner, device_id_type=MESH)

    row_id = lax.broadcasted_iota(jnp.int32, (group_rows, group_rows), 0)
    col_id = lax.broadcasted_iota(jnp.int32, (group_rows, group_rows), 1)
    wanted = (row_id % GROUP) * STRATA + row_id // GROUP
    picks = jnp.where(col_id == wanted, 1.0, 0.0).astype(jnp.bfloat16)

    def sort_group(group, carry):
        rows = pl.ds(pl.multiple_of(group * group_rows, group_rows), group_rows)
        there = pl.ds(pl.multiple_of(group * GROUP, GROUP), GROUP)
        for which in range(2):
            load(group, which).wait()
            by_stratum = jnp.dot(
                picks, raw[which, rows, :], preferred_element_type=jnp.float32
            ).astype(jnp.bfloat16)
            for stratum in range(STRATA):
                sorted_rows[which, stratum, there, :] = by_stratum[
                    stratum * GROUP : (stratum + 1) * GROUP
                ]
        return carry

    lax.fori_loop(0, groups, sort_group, 0)
    user_load.wait()
    item_load.wait()
    user_half[...] = user[...].astype(jnp.bfloat16)
    pl.semaphore_wait(barrier, 4)

    def move(stratum, piece):
        is_outer = (stratum == S_IN - 1).astype(jnp.int32)
        rows = pl.ds(piece * width, width)
        return pltpu.make_async_remote_copy(
            src_ref=fresh.at[stratum, rows],
            dst_ref=held.at[stratum + 1, rows],
            send_sem=send_sem.at[stratum, piece],
            recv_sem=recv_sem.at[stratum, piece],
            device_id=along(is_outer, 1 - is_outer),
            device_id_type=MESH,
        )

    def work(stratum, first, last):
        scales = listed_scales(list_ref, count_ref, stratum, tile_total)
        column = lax.broadcasted_iota(jnp.int32, (1, width), 1)
        for piece in range(PIECES):
            rows = slice(piece * width, (piece + 1) * width)
            if not first:
                move(stratum - 1, piece).wait_recv()
            item = held[stratum, rows, :]
            item_half = item.astype(jnp.bfloat16)
            listed = jnp.zeros((1, width), jnp.float32)
            for tile in range(width // tile_width):
                listed = jnp.where(
                    column >= tile * tile_width,
                    scales[piece * width // tile_width + tile],
                    listed,
                )
            predicted = lax.dot_general(
                user_half[...],
                item_half,
                (((1,), (1,)), ((), ())),
                preferred_element_type=jnp.float32,
            )
            rating = sorted_rows[0, stratum, :, rows].astype(jnp.float32)
            weight = sorted_rows[1, stratum, :, rows].astype(jnp.float32)
            residual = (weight * (predicted - rating) * listed).astype(jnp.bfloat16)
            grad_item = lax.dot_general(
                residual,
                user_half[...],
                (((0,), (0,)), ((), ())),
                preferred_element_type=jnp.float32,
            )
            fresh[stratum, rows, :] = item - learn_rate * (grad_item + ridge_weight * item)
            if last:
                pltpu.make_async_copy(
                    fresh.at[stratum, rows], item_out.at[rows], send_sem.at[stratum, piece]
                ).start()
            else:
                move(stratum, piece).start()
            part = jnp.dot(residual, item_half, preferred_element_type=jnp.float32)
            if piece == 0:
                grad_user[...] = part
            else:
                part = grad_user[...] + part
                if piece < PIECES - 1:
                    grad_user[...] = part
                else:
                    old = user[...]
                    new = old - learn_rate * (part + ridge_weight * old)
                    user[...] = new
                    if not last:
                        user_half[...] = new.astype(jnp.bfloat16)

    work(jnp.int32(0), True, False)

    def middle(stratum, carry):
        work(stratum, False, False)
        return carry

    lax.fori_loop(1, STRATA - 1, middle, 0)
    work(jnp.int32(STRATA - 1), False, True)

    user_store = pltpu.make_async_copy(user, user_out, factor_sem.at[0])
    user_store.start()
    for piece in range(PIECES):
        rows = slice(piece * width, (piece + 1) * width)
        pltpu.make_async_copy(
            fresh.at[STRATA - 1, rows], item_out.at[rows], send_sem.at[STRATA - 1, piece]
        ).wait()

    def sent(stratum, carry):
        for piece in range(PIECES):
            move(stratum, piece).wait_send()
        return carry

    lax.fori_loop(0, STRATA - 1, sent, 0)
    user_store.wait()


def local(outer_size, inner_size, user_factors, item_factors, ratings, weights, tile_list, tile_count):
    users, strata, items = ratings.shape
    rank = user_factors.shape[1]
    smem = pl.BlockSpec(memory_space=pltpu.SMEM)
    anywhere = pl.BlockSpec(memory_space=pl.ANY)
    block = jax.ShapeDtypeStruct((users, rank), jnp.float32)
    return pl.pallas_call(
        functools.partial(kernel, outer_size, inner_size),
        out_shape=(block, jax.ShapeDtypeStruct((items, rank), jnp.float32)),
        in_specs=[smem, smem, anywhere, anywhere, anywhere, anywhere],
        out_specs=(anywhere, anywhere),
        scratch_shapes=[
            pltpu.VMEM((2, users * strata, items), jnp.bfloat16),
            pltpu.VMEM((2, strata, users, items), jnp.bfloat16),
            pltpu.VMEM((users, rank), jnp.float32),
            pltpu.VMEM((users, rank), jnp.bfloat16),
            pltpu.VMEM((users, rank), jnp.float32),
            pltpu.VMEM((strata, items, rank), jnp.float32),
            pltpu.VMEM((strata, items, rank), jnp.float32),
            pltpu.SemaphoreType.DMA((2, users // GROUP)),
            pltpu.SemaphoreType.DMA((2,)),
            pltpu.SemaphoreType.DMA((strata, PIECES)),
            pltpu.SemaphoreType.DMA((strata, PIECES)),
        ],
        compiler_params=pltpu.CompilerParams(
            collective_id=0,
            has_side_effects=True,
            vmem_limit_bytes=48 * 1024 * 1024,
        ),
        cost_estimate=pl.CostEstimate(
            flops=3 * 2 * strata * users * items * rank,
            bytes_accessed=4 * users * strata * items + 16 * users * rank,
            transcendentals=0,
        ),
    )(
        tile_list,
        tile_count,
        user_factors,
        item_factors,
        ratings.reshape(users * strata, items),
        weights.reshape(users * strata, items),
    )


def solution(mesh):
    in_specs = (
        P(("outer", "inner"), None),
        P(("outer", "inner"), None),
        P(("outer", "inner"), None, None),
        P(("outer", "inner"), None, None),
        P(("outer", "inner"), None, None),
        P(("outer", "inner"), None),
    )
    out_specs = (P(("outer", "inner"), None), P(("outer", "inner"), None))
    return jax.shard_map(
        functools.partial(local, mesh.shape["outer"], mesh.shape["inner"]),
        mesh=mesh,
        in_specs=in_specs,
        out_specs=out_specs,
        check_vma=False,
    )
```

```python
import functools

import jax
import jax.numpy as jnp
from jax import lax
from jax.experimental import pallas as pl
from jax.experimental.pallas import tpu as pltpu
from jax.sharding import PartitionSpec as P

S_OUT = 2
S_IN = 4
STRATA = S_OUT * S_IN
GROUP = 32
CHIPS = 4
CORES = 2
PIECES = 2
PARTS = 4

learn_rate = 0.015
ridge_weight = 0.05

MESH = pl.DeviceIdType.MESH


def listed_scales(list_ref, count_ref, stratum, tile_total):
    count = count_ref[0, stratum]
    scales = []
    for tile in range(tile_total):
        hits = [
            jnp.where(
                (list_ref[0, slot, stratum] == tile) & (slot < count), 1.0, 0.0
            ).astype(jnp.float32)
            for slot in range(tile_total)
        ]
        scales.append(functools.reduce(jnp.maximum, hits))
    return scales


def kernel(
    outer_size,
    inner_size,
    list_hbm,
    count_hbm,
    user_hbm,
    item_hbm,
    rating_hbm,
    weight_hbm,
    user_out,
    item_out,
    list_ref,
    count_ref,
    raw,
    ordered,
    picks,
    user,
    user_half,
    grad_user,
    held,
    fresh,
    passing,
    load_sem,
    factor_sem,
    send_sem,
    recv_sem,
    pass_sem,
):
    users, rank = user.shape
    items = held.shape[1]
    width = items // PIECES
    tile_total = list_ref.shape[1]
    tile_width = items // tile_total
    groups = users // GROUP
    group_rows = GROUP * STRATA
    part_users = users // PARTS
    part_rows = part_users * STRATA

    g = lax.axis_index("outer")
    i = lax.axis_index("inner")

    run = CHIPS * CORES
    place = lax.rem(i, run)
    corner, stop = place == run - 1, place == run - 1 - CORES

    def along(steps_outer, steps_inner):
        return (
            lax.rem(g + steps_outer + outer_size, outer_size),
            lax.rem(i + steps_inner + inner_size, inner_size),
        )

    def load(which, piece, part):
        rows = pl.ds(part * part_rows, part_rows)
        cols = pl.ds(piece * width, width)
        source = (rating_hbm, weight_hbm)[which]
        return pltpu.make_async_copy(
            source.at[rows, cols], raw.at[which, rows, cols], load_sem.at[which, piece, part]
        )

    factor_loads = [
        pltpu.make_async_copy(list_hbm, list_ref, factor_sem.at[2]),
        pltpu.make_async_copy(count_hbm, count_ref, factor_sem.at[3]),
        pltpu.make_async_copy(user_hbm, user, factor_sem.at[0]),
        pltpu.make_async_copy(item_hbm, held.at[0], factor_sem.at[1]),
    ]
    for copy in factor_loads:
        copy.start()
    for piece in range(PIECES):
        for part in range(PARTS):
            load(0, piece, part).start()
            load(1, piece, part).start()

    barrier = pltpu.get_barrier_semaphore()
    for partner in (along(0, 1), along(0, -1), along(1, 0), along(-1, 0)):
        pl.semaphore_signal(barrier, inc=1, device_id=partner, device_id_type=MESH)

    @pl.when(corner)
    def greet_stop():
        pl.semaphore_signal(
            barrier, inc=1, device_id=along(-1, -CORES), device_id_type=MESH
        )

    @pl.when(stop)
    def greet_corner():
        pl.semaphore_signal(
            barrier, inc=1, device_id=along(0, CORES), device_id_type=MESH
        )

    def meet_all():
        @pl.when(corner | stop)
        def meet_five():
            pl.semaphore_wait(barrier, 5)

        @pl.when(jnp.logical_not(corner | stop))
        def meet_four():
            pl.semaphore_wait(barrier, 4)

    row_id = lax.broadcasted_iota(jnp.int32, (GROUP, group_rows), 0)
    col_id = lax.broadcasted_iota(jnp.int32, (GROUP, group_rows), 1)
    for stratum in range(STRATA):
        picks[stratum] = jnp.where(
            col_id == row_id * STRATA + stratum, 1.0, 0.0
        ).astype(jnp.bfloat16)

    def sort_part(stratum, part, cols):
        pick = picks[stratum]
        for group in range(groups // PARTS):
            base = part * part_rows + group * group_rows
            rows = pl.ds(pl.multiple_of(base, group_rows), group_rows)
            base = part * part_users + group * GROUP
            there = pl.ds(pl.multiple_of(base, GROUP), GROUP)
            for which in range(2):
                ordered[which, there, cols] = jnp.dot(
                    pick, raw[which, rows, cols], preferred_element_type=jnp.float32
                )

    def sort_all(stratum):
        def body(part, carry):
            sort_part(stratum, part, slice(None))
            return carry

        lax.fori_loop(0, PARTS, body, 0)

    def move(stratum, piece):
        is_outer = (stratum == S_IN - 1).astype(jnp.int32)
        rows = pl.ds(piece * width, width)
        return pltpu.make_async_remote_copy(
            src_ref=fresh.at[stratum, rows],
            dst_ref=held.at[stratum + 1, rows],
            send_sem=send_sem.at[stratum, piece],
            recv_sem=recv_sem.at[stratum, piece],
            device_id=along(is_outer, 1 - is_outer),
            device_id_type=MESH,
        )

    first_rows = pl.ds(0, width)
    turn = S_IN - 1

    def to_stop():
        return pltpu.make_async_remote_copy(
            src_ref=fresh.at[turn, first_rows],
            dst_ref=passing,
            send_sem=send_sem.at[turn, 0],
            recv_sem=pass_sem.at[0],
            device_id=along(0, -CORES),
            device_id_type=MESH,
        )

    def from_stop():
        return pltpu.make_async_remote_copy(
            src_ref=passing,
            dst_ref=held.at[turn + 1, first_rows],
            send_sem=pass_sem.at[1],
            recv_sem=recv_sem.at[turn, 0],
            device_id=along(1, CORES),
            device_id_type=MESH,
        )

    def send(stratum, piece):
        if piece == 0:
            around = corner & (stratum == turn)

            @pl.when(around)
            def send_around():
                to_stop().start()

            @pl.when(jnp.logical_not(around))
            def send_straight():
                move(stratum, piece).start()
        else:
            @pl.when((stratum == turn) & (place == run - 1))
            def yield_link():
                for earlier in range(PIECES):
                    move(stratum - 1, earlier).wait_send()

            move(stratum, piece).start()

    def work(stratum, first, last):
        scales = []
        if not first:
            scales.extend(listed_scales(list_ref, count_ref, stratum, tile_total))
        column = lax.broadcasted_iota(jnp.int32, (1, width), 1)
        for piece in range(PIECES):
            rows = slice(piece * width, (piece + 1) * width)
            if first:
                for part in range(PARTS):
                    load(0, piece, part).wait()
                    load(1, piece, part).wait()
                    sort_part(stratum, part, rows)
                if piece == 0:
                    for copy in factor_loads:
                        copy.wait()
                    user_half[...] = user[...].astype(jnp.bfloat16)
                    scales.extend(listed_scales(list_ref, count_ref, stratum, tile_total))
            else:
                move(stratum - 1, piece).wait_recv()
            item = held[stratum, rows, :]
            item_half = item.astype(jnp.bfloat16)
            listed = jnp.zeros((1, width), jnp.float32)
            for tile in range(width // tile_width):
                listed = jnp.where(
                    column >= tile * tile_width,
                    scales[piece * width // tile_width + tile],
                    listed,
                )
            predicted = lax.dot_general(
                user_half[...],
                item_half,
                (((1,), (1,)), ((), ())),
                preferred_element_type=jnp.float32,
            )
            rating = ordered[0, :, rows]
            weight = ordered[1, :, rows]
            residual = (weight * (predicted - rating) * listed).astype(jnp.bfloat16)
            grad_item = lax.dot_general(
                residual,
                user_half[...],
                (((0,), (0,)), ((), ())),
                preferred_element_type=jnp.float32,
            )
            fresh[stratum, rows, :] = item - learn_rate * (grad_item + ridge_weight * item)
            if last:
                pltpu.make_async_copy(
                    fresh.at[stratum, rows], item_out.at[rows], send_sem.at[stratum, piece]
                ).start()
            else:
                if first and piece == 0:
                    meet_all()
                send(stratum, piece)
            part = jnp.dot(residual, item_half, preferred_element_type=jnp.float32)
            if piece == 0:
                grad_user[...] = part
            else:
                part = grad_user[...] + part
                if piece < PIECES - 1:
                    grad_user[...] = part
                else:
                    old = user[...]
                    new = old - learn_rate * (part + ridge_weight * old)
                    user[...] = new
                    if not last:
                        user_half[...] = new.astype(jnp.bfloat16)
                        sort_all(stratum + 1)
                        if not first:

                            @pl.when(stop & (stratum == turn))
                            def pass_on():
                                to_stop().wait_recv()
                                from_stop().start()

    work(jnp.int32(0), True, False)

    def middle(stratum, carry):
        work(stratum, False, False)
        return carry

    lax.fori_loop(1, STRATA - 1, middle, 0)
    work(jnp.int32(STRATA - 1), False, True)

    user_store = pltpu.make_async_copy(user, user_out, factor_sem.at[0])
    user_store.start()
    for piece in range(PIECES):
        rows = slice(piece * width, (piece + 1) * width)
        pltpu.make_async_copy(
            fresh.at[STRATA - 1, rows], item_out.at[rows], send_sem.at[STRATA - 1, piece]
        ).wait()

    def sent(stratum, carry):
        @pl.when(jnp.logical_not((stratum == turn - 1) & (place == run - 1)))
        def settle():
            for piece in range(PIECES):
                move(stratum, piece).wait_send()

        return carry

    lax.fori_loop(0, STRATA - 1, sent, 0)

    @pl.when(stop)
    def settle_passed():
        from_stop().wait_send()

    user_store.wait()


def local(outer_size, inner_size, user_factors, item_factors, ratings, weights, tile_list, tile_count):
    users, strata, items = ratings.shape
    rank = user_factors.shape[1]
    anywhere = pl.BlockSpec(memory_space=pl.ANY)
    block = jax.ShapeDtypeStruct((users, rank), jnp.float32)
    return pl.pallas_call(
        functools.partial(kernel, outer_size, inner_size),
        out_shape=(block, jax.ShapeDtypeStruct((items, rank), jnp.float32)),
        in_specs=[anywhere] * 6,
        out_specs=(anywhere, anywhere),
        scratch_shapes=[
            pltpu.SMEM((1, tile_list.shape[2], strata), jnp.int32),
            pltpu.SMEM((1, strata), jnp.int32),
            pltpu.VMEM((2, users * strata, items), jnp.bfloat16),
            pltpu.VMEM((2, users, items), jnp.float32),
            pltpu.VMEM((strata, GROUP, GROUP * strata), jnp.bfloat16),
            pltpu.VMEM((users, rank), jnp.float32),
            pltpu.VMEM((users, rank), jnp.bfloat16),
            pltpu.VMEM((users, rank), jnp.float32),
            pltpu.VMEM((strata, items, rank), jnp.float32),
            pltpu.VMEM((strata, items, rank), jnp.float32),
            pltpu.VMEM((items // PIECES, rank), jnp.float32),
            pltpu.SemaphoreType.DMA((2, PIECES, PARTS)),
            pltpu.SemaphoreType.DMA((4,)),
            pltpu.SemaphoreType.DMA((strata, PIECES)),
            pltpu.SemaphoreType.DMA((strata, PIECES)),
            pltpu.SemaphoreType.DMA((2,)),
        ],
        compiler_params=pltpu.CompilerParams(
            collective_id=0,
            has_side_effects=True,
            vmem_limit_bytes=60 * 1024 * 1024,
        ),
        cost_estimate=pl.CostEstimate(
            flops=3 * 2 * strata * users * items * rank,
            bytes_accessed=4 * users * strata * items + 16 * users * rank,
            transcendentals=0,
        ),
    )(
        jnp.swapaxes(tile_list, 1, 2),
        tile_count,
        user_factors,
        item_factors,
        ratings.reshape(users * strata, items),
        weights.reshape(users * strata, items),
    )


def solution(mesh):
    in_specs = (
        P(("outer", "inner"), None),
        P(("outer", "inner"), None),
        P(("outer", "inner"), None, None),
        P(("outer", "inner"), None, None),
        P(("outer", "inner"), None, None),
        P(("outer", "inner"), None),
    )
    out_specs = (P(("outer", "inner"), None), P(("outer", "inner"), None))
    return jax.shard_map(
        functools.partial(local, mesh.shape["outer"], mesh.shape["inner"]),
        mesh=mesh,
        in_specs=in_specs,
        out_specs=out_specs,
        check_vma=False,
    )
```

```python
import functools

import jax
import jax.numpy as jnp
from jax import lax
from jax.experimental import pallas as pl
from jax.experimental.pallas import tpu as pltpu
from jax.sharding import PartitionSpec as P

S_OUT = 2
S_IN = 4
STRATA = S_OUT * S_IN
GROUP = 32
CHIPS = 4
CORES = 2
PIECES = 2
PARTS = 4

learn_rate = 0.015
ridge_weight = 0.05

MESH = pl.DeviceIdType.MESH


def listed_scales(list_ref, count_ref, stratum, tile_total):
    count = count_ref[0, stratum]
    scales = []
    for tile in range(tile_total):
        hits = [
            jnp.where(
                (list_ref[0, slot, stratum] == tile) & (slot < count), 1.0, 0.0
            ).astype(jnp.float32)
            for slot in range(tile_total)
        ]
        scales.append(functools.reduce(jnp.maximum, hits))
    return scales


def kernel(
    outer_size,
    inner_size,
    list_hbm,
    count_hbm,
    user_hbm,
    item_hbm,
    rating_hbm,
    weight_hbm,
    user_out,
    item_out,
    list_ref,
    count_ref,
    raw,
    ordered,
    picks,
    user,
    user_half,
    grad_user,
    held,
    fresh,
    passing,
    load_sem,
    factor_sem,
    send_sem,
    recv_sem,
    pass_sem,
    go_sem,
):
    users, rank = user.shape
    items = held.shape[1]
    width = items // PIECES
    tile_total = list_ref.shape[1]
    tile_width = items // tile_total
    groups = users // GROUP
    group_rows = GROUP * STRATA
    part_users = users // PARTS
    part_rows = part_users * STRATA

    g = lax.axis_index("outer")
    i = lax.axis_index("inner")

    run = CHIPS * CORES
    place = lax.rem(i, run)
    corner, stop = place == run - 1, place == run - 1 - CORES

    def along(steps_outer, steps_inner):
        return (
            lax.rem(g + steps_outer + outer_size, outer_size),
            lax.rem(i + steps_inner + inner_size, inner_size),
        )

    def load(which, piece, part):
        rows = pl.ds(part * part_rows, part_rows)
        cols = pl.ds(piece * width, width)
        source = (rating_hbm, weight_hbm)[which]
        return pltpu.make_async_copy(
            source.at[rows, cols], raw.at[which, rows, cols], load_sem.at[which, piece, part]
        )

    factor_loads = [
        pltpu.make_async_copy(list_hbm, list_ref, factor_sem.at[2]),
        pltpu.make_async_copy(count_hbm, count_ref, factor_sem.at[3]),
        pltpu.make_async_copy(user_hbm, user, factor_sem.at[0]),
        pltpu.make_async_copy(item_hbm, held.at[0], factor_sem.at[1]),
    ]
    for copy in factor_loads:
        copy.start()
    for piece in range(PIECES):
        for part in range(PARTS):
            load(0, piece, part).start()
            load(1, piece, part).start()

    barrier = pltpu.get_barrier_semaphore()
    for partner in (along(0, 1), along(0, -1), along(1, 0), along(-1, 0)):
        pl.semaphore_signal(barrier, inc=1, device_id=partner, device_id_type=MESH)

    @pl.when(corner)
    def greet_stop():
        pl.semaphore_signal(
            barrier, inc=1, device_id=along(-1, -CORES), device_id_type=MESH
        )

    @pl.when(stop)
    def greet_corner():
        pl.semaphore_signal(
            barrier, inc=1, device_id=along(0, CORES), device_id_type=MESH
        )

    def meet_all():
        @pl.when(corner | stop)
        def meet_five():
            pl.semaphore_wait(barrier, 5)

        @pl.when(jnp.logical_not(corner | stop))
        def meet_four():
            pl.semaphore_wait(barrier, 4)

    row_id = lax.broadcasted_iota(jnp.int32, (GROUP, group_rows), 0)
    col_id = lax.broadcasted_iota(jnp.int32, (GROUP, group_rows), 1)
    for stratum in range(STRATA):
        picks[stratum] = jnp.where(
            col_id == row_id * STRATA + stratum, 1.0, 0.0
        ).astype(jnp.bfloat16)

    def sort_part(stratum, part, cols):
        pick = picks[stratum]
        for group in range(groups // PARTS):
            base = part * part_rows + group * group_rows
            rows = pl.ds(pl.multiple_of(base, group_rows), group_rows)
            base = part * part_users + group * GROUP
            there = pl.ds(pl.multiple_of(base, GROUP), GROUP)
            for which in range(2):
                ordered[which, there, cols] = jnp.dot(
                    pick, raw[which, rows, cols], preferred_element_type=jnp.float32
                )

    def sort_all(stratum):
        def body(part, carry):
            sort_part(stratum, part, slice(None))
            return carry

        lax.fori_loop(0, PARTS, body, 0)

    def move(stratum, piece):
        is_outer = (stratum == S_IN - 1).astype(jnp.int32)
        rows = pl.ds(piece * width, width)
        return pltpu.make_async_remote_copy(
            src_ref=fresh.at[stratum, rows],
            dst_ref=held.at[stratum + 1, rows],
            send_sem=send_sem.at[stratum, piece],
            recv_sem=recv_sem.at[stratum, piece],
            device_id=along(is_outer, 1 - is_outer),
            device_id_type=MESH,
        )

    first_rows = pl.ds(0, width)
    turn = S_IN - 1

    def to_stop():
        return pltpu.make_async_remote_copy(
            src_ref=fresh.at[turn, first_rows],
            dst_ref=passing,
            send_sem=send_sem.at[turn, 0],
            recv_sem=pass_sem.at[0],
            device_id=along(0, -CORES),
            device_id_type=MESH,
        )

    def from_stop():
        return pltpu.make_async_remote_copy(
            src_ref=passing,
            dst_ref=held.at[turn + 1, first_rows],
            send_sem=pass_sem.at[1],
            recv_sem=recv_sem.at[turn, 0],
            device_id=along(1, CORES),
            device_id_type=MESH,
        )

    def clear():
        pl.semaphore_signal(go_sem, inc=1, device_id=along(0, -1), device_id_type=MESH)

    def send(stratum, piece):
        if piece == 0:

            @pl.when((stratum == turn) & ((place == run - 2) | (place == run - 4)))
            def hold():
                pl.semaphore_wait(go_sem, 1)

            around = corner & (stratum == turn)

            @pl.when(around)
            def send_around():
                to_stop().start()

            @pl.when(jnp.logical_not(around))
            def send_straight():
                move(stratum, piece).start()
        else:
            @pl.when((stratum == turn) & (place == run - 1))
            def yield_link():
                for earlier in range(PIECES):
                    move(stratum - 1, earlier).wait_send()

            move(stratum, piece).start()

    def work(stratum, first, last):
        scales = []
        if not first:
            scales.extend(listed_scales(list_ref, count_ref, stratum, tile_total))
        column = lax.broadcasted_iota(jnp.int32, (1, width), 1)
        for piece in range(PIECES):
            rows = slice(piece * width, (piece + 1) * width)
            if first:
                for part in range(PARTS):
                    load(0, piece, part).wait()
                    load(1, piece, part).wait()
                    sort_part(stratum, part, rows)
                if piece == 0:
                    for copy in factor_loads:
                        copy.wait()
                    user_half[...] = user[...].astype(jnp.bfloat16)
                    scales.extend(listed_scales(list_ref, count_ref, stratum, tile_total))
            else:
                move(stratum - 1, piece).wait_recv()
            item = held[stratum, rows, :]
            item_half = item.astype(jnp.bfloat16)
            listed = jnp.zeros((1, width), jnp.float32)
            for tile in range(width // tile_width):
                listed = jnp.where(
                    column >= tile * tile_width,
                    scales[piece * width // tile_width + tile],
                    listed,
                )
            predicted = lax.dot_general(
                user_half[...],
                item_half,
                (((1,), (1,)), ((), ())),
                preferred_element_type=jnp.float32,
            )
            rating = ordered[0, :, rows]
            weight = ordered[1, :, rows]
            residual = (weight * (predicted - rating) * listed).astype(jnp.bfloat16)
            grad_item = lax.dot_general(
                residual,
                user_half[...],
                (((0,), (0,)), ((), ())),
                preferred_element_type=jnp.float32,
            )
            renewed = item - learn_rate * (grad_item + ridge_weight * item)
            if last:
                item_out[rows, :] = renewed
            else:
                fresh[stratum, rows, :] = renewed
                if first and piece == 0:
                    meet_all()
                send(stratum, piece)
            part = jnp.dot(residual, item_half, preferred_element_type=jnp.float32)
            if piece == 0:
                grad_user[...] = part
            else:
                part = grad_user[...] + part
                if piece < PIECES - 1:
                    grad_user[...] = part
                else:
                    old = user[...]
                    new = old - learn_rate * (part + ridge_weight * old)
                    if last:
                        user_out[...] = new
                    else:
                        user[...] = new
                        user_half[...] = new.astype(jnp.bfloat16)
                        sort_all(stratum + 1)
                        if not first:

                            @pl.when(corner & (stratum == turn))
                            def clear_row():
                                move(stratum, 1).wait_send()
                                clear()

                            @pl.when(stop & (stratum == turn))
                            def pass_on():
                                to_stop().wait_recv()
                                from_stop().start()
                                from_stop().wait_send()
                                clear()

    work(jnp.int32(0), True, False)

    def middle(stratum, carry):
        work(stratum, False, False)
        return carry

    lax.fori_loop(1, STRATA - 1, middle, 0)
    work(jnp.int32(STRATA - 1), False, True)

    def sent(stratum, carry):
        @pl.when(jnp.logical_not((stratum == turn - 1) & (place == run - 1)))
        def settle():
            move(stratum, 0).wait_send()

            @pl.when(jnp.logical_not((stratum == turn) & corner))
            def settle_rest():
                move(stratum, 1).wait_send()

        return carry

    lax.fori_loop(0, STRATA - 1, sent, 0)


def local(outer_size, inner_size, user_factors, item_factors, ratings, weights, tile_list, tile_count):
    users, strata, items = ratings.shape
    rank = user_factors.shape[1]
    anywhere = pl.BlockSpec(memory_space=pl.ANY)
    block = pltpu.VMEM((users, rank), jnp.float32)
    return pl.pallas_call(
        functools.partial(kernel, outer_size, inner_size),
        out_shape=(block, pltpu.VMEM((items, rank), jnp.float32)),
        in_specs=[anywhere] * 6,
        out_specs=(pl.BlockSpec(memory_space=pltpu.VMEM),) * 2,
        scratch_shapes=[
            pltpu.SMEM((1, tile_list.shape[2], strata), jnp.int32),
            pltpu.SMEM((1, strata), jnp.int32),
            pltpu.VMEM((2, users * strata, items), jnp.bfloat16),
            pltpu.VMEM((2, users, items), jnp.float32),
            pltpu.VMEM((strata, GROUP, GROUP * strata), jnp.bfloat16),
            pltpu.VMEM((users, rank), jnp.float32),
            pltpu.VMEM((users, rank), jnp.bfloat16),
            pltpu.VMEM((users, rank), jnp.float32),
            pltpu.VMEM((strata, items, rank), jnp.float32),
            pltpu.VMEM((strata, items, rank), jnp.float32),
            pltpu.VMEM((items // PIECES, rank), jnp.float32),
            pltpu.SemaphoreType.DMA((2, PIECES, PARTS)),
            pltpu.SemaphoreType.DMA((4,)),
            pltpu.SemaphoreType.DMA((strata, PIECES)),
            pltpu.SemaphoreType.DMA((strata, PIECES)),
            pltpu.SemaphoreType.DMA((2,)),
            pltpu.SemaphoreType.REGULAR,
        ],
        compiler_params=pltpu.CompilerParams(
            collective_id=0,
            has_side_effects=True,
            vmem_limit_bytes=40 * 1024 * 1024,
        ),
        cost_estimate=pl.CostEstimate(
            flops=3 * 2 * strata * users * items * rank,
            bytes_accessed=4 * users * strata * items + 16 * users * rank,
            transcendentals=0,
        ),
    )(
        *[
            pltpu.with_memory_space_constraint(operand, pltpu.HBM)
            for operand in (
                jnp.swapaxes(tile_list, 1, 2),
                tile_count,
                user_factors,
                item_factors,
                ratings.reshape(users * strata, items),
                weights.reshape(users * strata, items),
            )
        ]
    )


def solution(mesh):
    in_specs = (
        P(("outer", "inner"), None),
        P(("outer", "inner"), None),
        P(("outer", "inner"), None, None),
        P(("outer", "inner"), None, None),
        P(("outer", "inner"), None, None),
        P(("outer", "inner"), None),
    )
    out_specs = (P(("outer", "inner"), None), P(("outer", "inner"), None))
    return jax.shard_map(
        functools.partial(local, mesh.shape["outer"], mesh.shape["inner"]),
        mesh=mesh,
        in_specs=in_specs,
        out_specs=out_specs,
        check_vma=False,
    )
```

```python
import functools

import jax
import jax.numpy as jnp
from jax import lax
from jax.experimental import pallas as pl
from jax.experimental.pallas import tpu as pltpu
from jax.sharding import PartitionSpec as P

S_OUT = 2
S_IN = 4
STRATA = S_OUT * S_IN
GROUP = 32
CHIPS = 4
CORES = 2
PIECES = 2
PARTS = 2

learn_rate = 0.015
ridge_weight = 0.05

MESH = pl.DeviceIdType.MESH


def listed_scales(list_ref, count_ref, stratum, tile_total):
    count = count_ref[0, stratum]
    scales = []
    for tile in range(tile_total):
        hits = [
            jnp.where(
                (list_ref[0, slot, stratum] == tile) & (slot < count), 1.0, 0.0
            ).astype(jnp.float32)
            for slot in range(tile_total)
        ]
        scales.append(functools.reduce(jnp.maximum, hits))
    return scales


def kernel(
    outer_size,
    inner_size,
    list_hbm,
    count_hbm,
    user_hbm,
    item_hbm,
    rating_hbm,
    weight_hbm,
    user_out,
    item_out,
    list_ref,
    count_ref,
    raw,
    ordered,
    picks,
    user,
    user_half,
    grad_user,
    held,
    fresh,
    passing,
    load_sem,
    factor_sem,
    send_sem,
    recv_sem,
    pass_sem,
    go_sem,
):
    users, rank = user.shape
    items = held.shape[1]
    width = items // PIECES
    tile_total = list_ref.shape[1]
    tile_width = items // tile_total
    groups = users // GROUP
    group_rows = GROUP * STRATA
    part_users = users // PARTS
    part_rows = part_users * STRATA

    g = lax.axis_index("outer")
    i = lax.axis_index("inner")

    run = CHIPS * CORES
    place = lax.rem(i, run)
    corner, stop = place == run - 1, place == run - 1 - CORES

    def along(steps_outer, steps_inner):
        return (
            lax.rem(g + steps_outer + outer_size, outer_size),
            lax.rem(i + steps_inner + inner_size, inner_size),
        )

    def load(which, piece, part):
        rows = pl.ds(part * part_rows, part_rows)
        cols = pl.ds(piece * width, width)
        source = (rating_hbm, weight_hbm)[which]
        return pltpu.make_async_copy(
            source.at[rows, cols], raw.at[which, rows, cols], load_sem.at[which, piece, part]
        )

    factor_loads = [
        pltpu.make_async_copy(list_hbm, list_ref, factor_sem.at[2]),
        pltpu.make_async_copy(count_hbm, count_ref, factor_sem.at[3]),
        pltpu.make_async_copy(user_hbm, user, factor_sem.at[0]),
        pltpu.make_async_copy(item_hbm, held.at[0], factor_sem.at[1]),
    ]
    for copy in factor_loads:
        copy.start()
    for piece in range(PIECES):
        for part in range(PARTS):
            load(0, piece, part).start()
            load(1, piece, part).start()

    barrier = pltpu.get_barrier_semaphore()
    for partner in (along(0, 1), along(0, -1), along(1, 0), along(-1, 0)):
        pl.semaphore_signal(barrier, inc=1, device_id=partner, device_id_type=MESH)

    @pl.when(corner)
    def greet_stop():
        pl.semaphore_signal(
            barrier, inc=1, device_id=along(-1, -CORES), device_id_type=MESH
        )

    @pl.when(stop)
    def greet_corner():
        pl.semaphore_signal(
            barrier, inc=1, device_id=along(0, CORES), device_id_type=MESH
        )

    def meet_all():
        @pl.when(corner | stop)
        def meet_five():
            pl.semaphore_wait(barrier, 5)

        @pl.when(jnp.logical_not(corner | stop))
        def meet_four():
            pl.semaphore_wait(barrier, 4)

    row_id = lax.broadcasted_iota(jnp.int32, (GROUP, group_rows), 0)
    col_id = lax.broadcasted_iota(jnp.int32, (GROUP, group_rows), 1)
    for stratum in range(STRATA):
        picks[stratum] = jnp.where(
            col_id == row_id * STRATA + stratum, 1.0, 0.0
        ).astype(jnp.bfloat16)

    def sort_part(stratum, part, cols):
        pick = picks[stratum]
        for group in range(groups // PARTS):
            base = part * part_rows + group * group_rows
            rows = pl.ds(pl.multiple_of(base, group_rows), group_rows)
            base = part * part_users + group * GROUP
            there = pl.ds(pl.multiple_of(base, GROUP), GROUP)
            for which in range(2):
                ordered[which, there, cols] = jnp.dot(
                    pick, raw[which, rows, cols], preferred_element_type=jnp.float32
                )

    def sort_all(stratum):
        def body(part, carry):
            sort_part(stratum, part, slice(None))
            return carry

        lax.fori_loop(0, PARTS, body, 0)

    def move(stratum, piece):
        is_outer = (stratum == S_IN - 1).astype(jnp.int32)
        rows = pl.ds(piece * width, width)
        return pltpu.make_async_remote_copy(
            src_ref=fresh.at[stratum, rows],
            dst_ref=held.at[stratum + 1, rows],
            send_sem=send_sem.at[stratum, piece],
            recv_sem=recv_sem.at[stratum, piece],
            device_id=along(is_outer, 1 - is_outer),
            device_id_type=MESH,
        )

    first_rows = pl.ds(0, width)
    turn = S_IN - 1

    def to_stop():
        return pltpu.make_async_remote_copy(
            src_ref=fresh.at[turn, first_rows],
            dst_ref=passing,
            send_sem=send_sem.at[turn, 0],
            recv_sem=pass_sem.at[0],
            device_id=along(0, -CORES),
            device_id_type=MESH,
        )

    def from_stop():
        return pltpu.make_async_remote_copy(
            src_ref=passing,
            dst_ref=held.at[turn + 1, first_rows],
            send_sem=pass_sem.at[1],
            recv_sem=recv_sem.at[turn, 0],
            device_id=along(1, CORES),
            device_id_type=MESH,
        )

    def clear():
        pl.semaphore_signal(go_sem, inc=1, device_id=along(0, -1), device_id_type=MESH)

    def send(stratum, piece):
        if piece == 0:

            @pl.when((stratum == turn) & ((place == run - 4)))
            def hold():
                pl.semaphore_wait(go_sem, 1)

            around = corner & (stratum == turn)

            @pl.when(around)
            def send_around():
                to_stop().start()

            @pl.when(jnp.logical_not(around))
            def send_straight():
                move(stratum, piece).start()
        else:
            @pl.when((stratum == turn) & (place == run - 1))
            def yield_link():
                for earlier in range(PIECES):
                    move(stratum - 1, earlier).wait_send()

            move(stratum, piece).start()

    def work(stratum, first, last):
        scales = []
        if not first:
            scales.extend(listed_scales(list_ref, count_ref, stratum, tile_total))
        column = lax.broadcasted_iota(jnp.int32, (1, width), 1)
        for piece in range(PIECES):
            rows = slice(piece * width, (piece + 1) * width)
            if first:
                for part in range(PARTS):
                    load(0, piece, part).wait()
                    load(1, piece, part).wait()
                    sort_part(stratum, part, rows)
                if piece == 0:
                    for copy in factor_loads:
                        copy.wait()
                    user_half[...] = user[...].astype(jnp.bfloat16)
                    scales.extend(listed_scales(list_ref, count_ref, stratum, tile_total))
            else:
                move(stratum - 1, piece).wait_recv()
            item = held[stratum, rows, :]
            item_half = item.astype(jnp.bfloat16)
            listed = jnp.zeros((1, width), jnp.float32)
            for tile in range(width // tile_width):
                listed = jnp.where(
                    column >= tile * tile_width,
                    scales[piece * width // tile_width + tile],
                    listed,
                )
            predicted = lax.dot_general(
                user_half[...],
                item_half,
                (((1,), (1,)), ((), ())),
                preferred_element_type=jnp.float32,
            )
            rating = ordered[0, :, rows]
            weight = ordered[1, :, rows]
            residual = (weight * (predicted - rating) * listed).astype(jnp.bfloat16)
            grad_item = lax.dot_general(
                residual,
                user_half[...],
                (((0,), (0,)), ((), ())),
                preferred_element_type=jnp.float32,
            )
            renewed = item - learn_rate * (grad_item + ridge_weight * item)
            if last:
                item_out[rows, :] = renewed
            else:
                fresh[stratum, rows, :] = renewed
                if first and piece == 0:
                    meet_all()
                send(stratum, piece)
            part = jnp.dot(residual, item_half, preferred_element_type=jnp.float32)
            if piece == 0:
                grad_user[...] = part
            else:
                part = grad_user[...] + part
                if piece < PIECES - 1:
                    grad_user[...] = part
                else:
                    old = user[...]
                    new = old - learn_rate * (part + ridge_weight * old)
                    if last:
                        user_out[...] = new
                    else:
                        user[...] = new
                        user_half[...] = new.astype(jnp.bfloat16)
                        sort_all(stratum + 1)
                        if not first:

                            @pl.when(stop & (stratum == turn))
                            def pass_on():
                                to_stop().wait_recv()
                                from_stop().start()
                                from_stop().wait_send()
                                clear()

    work(jnp.int32(0), True, False)

    def middle(stratum, carry):
        work(stratum, False, False)
        return carry

    lax.fori_loop(1, STRATA - 1, middle, 0)
    work(jnp.int32(STRATA - 1), False, True)

    def sent(stratum, carry):
        @pl.when(jnp.logical_not((stratum == turn - 1) & (place == run - 1)))
        def settle():
            for piece in range(PIECES):
                move(stratum, piece).wait_send()

        return carry

    lax.fori_loop(0, STRATA - 1, sent, 0)


def local(outer_size, inner_size, user_factors, item_factors, ratings, weights, tile_list, tile_count):
    users, strata, items = ratings.shape
    rank = user_factors.shape[1]
    anywhere = pl.BlockSpec(memory_space=pl.ANY)
    block = pltpu.VMEM((users, rank), jnp.float32)
    return pl.pallas_call(
        functools.partial(kernel, outer_size, inner_size),
        out_shape=(block, pltpu.VMEM((items, rank), jnp.float32)),
        in_specs=[anywhere] * 6,
        out_specs=(pl.BlockSpec(memory_space=pltpu.VMEM),) * 2,
        scratch_shapes=[
            pltpu.SMEM((1, tile_list.shape[2], strata), jnp.int32),
            pltpu.SMEM((1, strata), jnp.int32),
            pltpu.VMEM((2, users * strata, items), jnp.bfloat16),
            pltpu.VMEM((2, users, items), jnp.float32),
            pltpu.VMEM((strata, GROUP, GROUP * strata), jnp.bfloat16),
            pltpu.VMEM((users, rank), jnp.float32),
            pltpu.VMEM((users, rank), jnp.bfloat16),
            pltpu.VMEM((users, rank), jnp.float32),
            pltpu.VMEM((strata, items, rank), jnp.float32),
            pltpu.VMEM((strata, items, rank), jnp.float32),
            pltpu.VMEM((items // PIECES, rank), jnp.float32),
            pltpu.SemaphoreType.DMA((2, PIECES, PARTS)),
            pltpu.SemaphoreType.DMA((4,)),
            pltpu.SemaphoreType.DMA((strata, PIECES)),
            pltpu.SemaphoreType.DMA((strata, PIECES)),
            pltpu.SemaphoreType.DMA((2,)),
            pltpu.SemaphoreType.REGULAR,
        ],
        compiler_params=pltpu.CompilerParams(
            collective_id=0,
            has_side_effects=True,
            vmem_limit_bytes=40 * 1024 * 1024,
        ),
        cost_estimate=pl.CostEstimate(
            flops=3 * 2 * strata * users * items * rank,
            bytes_accessed=4 * users * strata * items + 16 * users * rank,
            transcendentals=0,
        ),
    )(
        *[
            pltpu.with_memory_space_constraint(operand, pltpu.HBM)
            for operand in (
                jnp.swapaxes(tile_list, 1, 2),
                tile_count,
                user_factors,
                item_factors,
                ratings.reshape(users * strata, items),
                weights.reshape(users * strata, items),
            )
        ]
    )


def solution(mesh):
    in_specs = (
        P(("outer", "inner"), None),
        P(("outer", "inner"), None),
        P(("outer", "inner"), None, None),
        P(("outer", "inner"), None, None),
        P(("outer", "inner"), None, None),
        P(("outer", "inner"), None),
    )
    out_specs = (P(("outer", "inner"), None), P(("outer", "inner"), None))
    return jax.shard_map(
        functools.partial(local, mesh.shape["outer"], mesh.shape["inner"]),
        mesh=mesh,
        in_specs=in_specs,
        out_specs=out_specs,
        check_vma=False,
    )
```

```python
import functools

import jax
import jax.numpy as jnp
from jax import lax
from jax.experimental import pallas as pl
from jax.experimental.pallas import tpu as pltpu
from jax.sharding import PartitionSpec as P

S_OUT = 2
S_IN = 4
STRATA = S_OUT * S_IN
GROUP = 32
CHIPS = 4
CORES = 2
PIECES = 2
PARTS = 1

learn_rate = 0.015
ridge_weight = 0.05

MESH = pl.DeviceIdType.MESH


def listed_scales(list_ref, count_ref, stratum, tile_total):
    count = count_ref[0, stratum]
    scales = []
    for tile in range(tile_total):
        hits = [
            jnp.where(
                (list_ref[0, slot, stratum] == tile) & (slot < count), 1.0, 0.0
            ).astype(jnp.float32)
            for slot in range(tile_total)
        ]
        scales.append(functools.reduce(jnp.maximum, hits))
    return scales


def kernel(
    outer_size,
    inner_size,
    list_hbm,
    count_hbm,
    user_hbm,
    item_hbm,
    rating_hbm,
    weight_hbm,
    user_out,
    item_out,
    list_ref,
    count_ref,
    raw,
    ordered,
    picks,
    user,
    user_half,
    grad_user,
    held,
    fresh,
    passing,
    load_sem,
    factor_sem,
    send_sem,
    recv_sem,
    pass_sem,
    go_sem,
):
    users, rank = user.shape
    items = held.shape[1]
    width = items // PIECES
    tile_total = list_ref.shape[1]
    tile_width = items // tile_total
    groups = users // GROUP
    group_rows = GROUP * STRATA
    part_users = users // PARTS
    part_rows = part_users * STRATA

    g = lax.axis_index("outer")
    i = lax.axis_index("inner")

    run = CHIPS * CORES
    place = lax.rem(i, run)
    corner, stop = place == run - 1, place == run - 1 - CORES

    def along(steps_outer, steps_inner):
        return (
            lax.rem(g + steps_outer + outer_size, outer_size),
            lax.rem(i + steps_inner + inner_size, inner_size),
        )

    def load(which, piece, part):
        rows = pl.ds(part * part_rows, part_rows)
        cols = pl.ds(piece * width, width)
        source = (rating_hbm, weight_hbm)[which]
        return pltpu.make_async_copy(
            source.at[rows, cols], raw.at[which, rows, cols], load_sem.at[which, piece, part]
        )

    factor_loads = [
        pltpu.make_async_copy(list_hbm, list_ref, factor_sem.at[2]),
        pltpu.make_async_copy(count_hbm, count_ref, factor_sem.at[3]),
        pltpu.make_async_copy(user_hbm, user, factor_sem.at[0]),
        pltpu.make_async_copy(item_hbm, held.at[0], factor_sem.at[1]),
    ]
    for copy in factor_loads:
        copy.start()
    for piece in range(PIECES):
        for part in range(PARTS):
            load(0, piece, part).start()
            load(1, piece, part).start()

    barrier = pltpu.get_barrier_semaphore()
    for partner in (along(0, 1), along(0, -1), along(1, 0), along(-1, 0)):
        pl.semaphore_signal(barrier, inc=1, device_id=partner, device_id_type=MESH)

    @pl.when(corner)
    def greet_stop():
        pl.semaphore_signal(
            barrier, inc=1, device_id=along(-1, -CORES), device_id_type=MESH
        )

    @pl.when(stop)
    def greet_corner():
        pl.semaphore_signal(
            barrier, inc=1, device_id=along(0, CORES), device_id_type=MESH
        )

    def meet_all():
        @pl.when(corner | stop)
        def meet_five():
            pl.semaphore_wait(barrier, 5)

        @pl.when(jnp.logical_not(corner | stop))
        def meet_four():
            pl.semaphore_wait(barrier, 4)

    row_id = lax.broadcasted_iota(jnp.int32, (GROUP, group_rows), 0)
    col_id = lax.broadcasted_iota(jnp.int32, (GROUP, group_rows), 1)
    for stratum in range(STRATA):
        picks[stratum] = jnp.where(
            col_id == row_id * STRATA + stratum, 1.0, 0.0
        ).astype(jnp.bfloat16)

    def sort_part(stratum, part, cols):
        pick = picks[stratum]
        for group in range(groups // PARTS):
            base = part * part_rows + group * group_rows
            rows = pl.ds(pl.multiple_of(base, group_rows), group_rows)
            base = part * part_users + group * GROUP
            there = pl.ds(pl.multiple_of(base, GROUP), GROUP)
            for which in range(2):
                ordered[which, there, cols] = jnp.dot(
                    pick, raw[which, rows, cols], preferred_element_type=jnp.float32
                )

    def sort_all(stratum):
        def body(part, carry):
            sort_part(stratum, part, slice(None))
            return carry

        lax.fori_loop(0, PARTS, body, 0)

    def move(stratum, piece):
        is_outer = (stratum == S_IN - 1).astype(jnp.int32)
        rows = pl.ds(piece * width, width)
        return pltpu.make_async_remote_copy(
            src_ref=fresh.at[stratum, rows],
            dst_ref=held.at[stratum + 1, rows],
            send_sem=send_sem.at[stratum, piece],
            recv_sem=recv_sem.at[stratum, piece],
            device_id=along(is_outer, 1 - is_outer),
            device_id_type=MESH,
        )

    first_rows = pl.ds(0, width)
    turn = S_IN - 1

    def to_stop():
        return pltpu.make_async_remote_copy(
            src_ref=fresh.at[turn, first_rows],
            dst_ref=passing,
            send_sem=send_sem.at[turn, 0],
            recv_sem=pass_sem.at[0],
            device_id=along(0, -CORES),
            device_id_type=MESH,
        )

    def from_stop():
        return pltpu.make_async_remote_copy(
            src_ref=passing,
            dst_ref=held.at[turn + 1, first_rows],
            send_sem=pass_sem.at[1],
            recv_sem=recv_sem.at[turn, 0],
            device_id=along(1, CORES),
            device_id_type=MESH,
        )

    def clear():
        pl.semaphore_signal(go_sem, inc=1, device_id=along(0, -1), device_id_type=MESH)

    def send(stratum, piece):
        if piece == 0:

            @pl.when((stratum == turn) & ((place == run - 4)))
            def hold():
                pl.semaphore_wait(go_sem, 1)

            around = corner & (stratum == turn)

            @pl.when(around)
            def send_around():
                to_stop().start()

            @pl.when(jnp.logical_not(around))
            def send_straight():
                move(stratum, piece).start()
        else:
            @pl.when((stratum == turn) & (place == run - 1))
            def yield_link():
                for earlier in range(PIECES):
                    move(stratum - 1, earlier).wait_send()

            move(stratum, piece).start()

    def work(stratum, first, last):
        scales = []
        if not first:
            scales.extend(listed_scales(list_ref, count_ref, stratum, tile_total))
        column = lax.broadcasted_iota(jnp.int32, (1, width), 1)
        for piece in range(PIECES):
            rows = slice(piece * width, (piece + 1) * width)
            if first:
                for part in range(PARTS):
                    load(0, piece, part).wait()
                    load(1, piece, part).wait()
                    sort_part(stratum, part, rows)
                if piece == 0:
                    for copy in factor_loads:
                        copy.wait()
                    user_half[...] = user[...].astype(jnp.bfloat16)
                    scales.extend(listed_scales(list_ref, count_ref, stratum, tile_total))
            else:
                move(stratum - 1, piece).wait_recv()
            item = held[stratum, rows, :]
            item_half = item.astype(jnp.bfloat16)
            listed = jnp.zeros((1, width), jnp.float32)
            for tile in range(width // tile_width):
                listed = jnp.where(
                    column >= tile * tile_width,
                    scales[piece * width // tile_width + tile],
                    listed,
                )
            predicted = lax.dot_general(
                user_half[...],
                item_half,
                (((1,), (1,)), ((), ())),
                preferred_element_type=jnp.float32,
            )
            rating = ordered[0, :, rows]
            weight = ordered[1, :, rows]
            residual = (weight * (predicted - rating) * listed).astype(jnp.bfloat16)
            grad_item = lax.dot_general(
                residual,
                user_half[...],
                (((0,), (0,)), ((), ())),
                preferred_element_type=jnp.float32,
            )
            renewed = item - learn_rate * (grad_item + ridge_weight * item)
            if last:
                item_out[rows, :] = renewed
            else:
                fresh[stratum, rows, :] = renewed
                if first and piece == 0:
                    meet_all()
                send(stratum, piece)
            part = jnp.dot(residual, item_half, preferred_element_type=jnp.float32)
            if piece == 0:
                grad_user[...] = part
            else:
                part = grad_user[...] + part
                if piece < PIECES - 1:
                    grad_user[...] = part
                else:
                    old = user[...]
                    new = old - learn_rate * (part + ridge_weight * old)
                    if last:
                        user_out[...] = new
                    else:
                        user[...] = new
                        user_half[...] = new.astype(jnp.bfloat16)
                        sort_all(stratum + 1)
                        if not first:

                            @pl.when(stop & (stratum == turn))
                            def pass_on():
                                to_stop().wait_recv()
                                from_stop().start()
                                from_stop().wait_send()
                                clear()

    work(jnp.int32(0), True, False)

    def middle(stratum, carry):
        work(stratum, False, False)
        return carry

    lax.fori_loop(1, STRATA - 1, middle, 0)
    work(jnp.int32(STRATA - 1), False, True)

    def sent(stratum, carry):
        @pl.when(jnp.logical_not((stratum == turn - 1) & (place == run - 1)))
        def settle():
            for piece in range(PIECES):
                move(stratum, piece).wait_send()

        return carry

    lax.fori_loop(0, STRATA - 1, sent, 0)


def local(outer_size, inner_size, user_factors, item_factors, ratings, weights, tile_list, tile_count):
    users, strata, items = ratings.shape
    rank = user_factors.shape[1]
    anywhere = pl.BlockSpec(memory_space=pl.ANY)
    block = pltpu.VMEM((users, rank), jnp.float32)
    return pl.pallas_call(
        functools.partial(kernel, outer_size, inner_size),
        out_shape=(block, pltpu.VMEM((items, rank), jnp.float32)),
        in_specs=[anywhere] * 6,
        out_specs=(pl.BlockSpec(memory_space=pltpu.VMEM),) * 2,
        scratch_shapes=[
            pltpu.SMEM((1, tile_list.shape[2], strata), jnp.int32),
            pltpu.SMEM((1, strata), jnp.int32),
            pltpu.VMEM((2, users * strata, items), jnp.bfloat16),
            pltpu.VMEM((2, users, items), jnp.float32),
            pltpu.VMEM((strata, GROUP, GROUP * strata), jnp.bfloat16),
            pltpu.VMEM((users, rank), jnp.float32),
            pltpu.VMEM((users, rank), jnp.bfloat16),
            pltpu.VMEM((users, rank), jnp.float32),
            pltpu.VMEM((strata, items, rank), jnp.float32),
            pltpu.VMEM((strata, items, rank), jnp.float32),
            pltpu.VMEM((items // PIECES, rank), jnp.float32),
            pltpu.SemaphoreType.DMA((2, PIECES, PARTS)),
            pltpu.SemaphoreType.DMA((4,)),
            pltpu.SemaphoreType.DMA((strata, PIECES)),
            pltpu.SemaphoreType.DMA((strata, PIECES)),
            pltpu.SemaphoreType.DMA((2,)),
            pltpu.SemaphoreType.REGULAR,
        ],
        compiler_params=pltpu.CompilerParams(
            collective_id=0,
            has_side_effects=True,
            vmem_limit_bytes=40 * 1024 * 1024,
        ),
        cost_estimate=pl.CostEstimate(
            flops=3 * 2 * strata * users * items * rank,
            bytes_accessed=4 * users * strata * items + 16 * users * rank,
            transcendentals=0,
        ),
    )(
        *[
            pltpu.with_memory_space_constraint(operand, pltpu.HBM)
            for operand in (
                jnp.swapaxes(tile_list, 1, 2),
                tile_count,
                user_factors,
                item_factors,
                ratings.reshape(users * strata, items),
                weights.reshape(users * strata, items),
            )
        ]
    )


def solution(mesh):
    in_specs = (
        P(("outer", "inner"), None),
        P(("outer", "inner"), None),
        P(("outer", "inner"), None, None),
        P(("outer", "inner"), None, None),
        P(("outer", "inner"), None, None),
        P(("outer", "inner"), None),
    )
    out_specs = (P(("outer", "inner"), None), P(("outer", "inner"), None))
    return jax.shard_map(
        functools.partial(local, mesh.shape["outer"], mesh.shape["inner"]),
        mesh=mesh,
        in_specs=in_specs,
        out_specs=out_specs,
        check_vma=False,
    )
```
